256 devices in a mesh: ctx: 32 (over x, y, core), head: 8 (over z).
Axes of the slice: x: 4, y: 4, z: 8, core: 2. Of those that a mesh axis runs over, the one named last changes fastest.
Arguments:
- queries: bfloat16 [24576, 8192], P('ctx', 'head'), may hold values from -80 to 80
- key_states: bfloat16 [24576, 8192], P('ctx', 'head'), may hold values from -4 to 4
- value_states: bfloat16 [24576, 8192], P('ctx', 'head'), may hold values from -4 to 4
- selection: int32 [512, 2], P('ctx'), may hold values from -1 to 30, as said below
Outputs:
- attended: bfloat16 [24576, 8192], P(('ctx', 'head'))
The draws below stay inside these ranges and needn't reach their ends.
Inputs may be any that keep to these rules, and one draw needn't show every extreme that they name: For query block b, the rows b * 16 to (b + 1) * 16 - 1 of selection, read row by row, list each of the blocks 0 to b - 1 exactly once in their first b entries, in an order drawn from the seed; all other entries are -1. So no two tiles of one query block list the same key block, and each query block from 1 on lists block 0.
All inputs are finite; a program needn't handle non-finite values.
Results may differ from the reference program's by a relative error of at most 0.0051.
Values may be sent and summed in bfloat16 or wider, within the bound.
A program may use at most 128 MiB of HBM per device.

```python
import math
import jax
import jax.numpy as jnp
from jax import lax

HEADS = 64
HEAD_DIM = 128
BLOCK = 768
PICKS = 2
TOKENS = 24576
TILES_BLK = 16
TILE = 48
N_CTX = 32


def key_base(key):
    return jnp.clip(jax.random.normal(key, (TOKENS, HEADS * HEAD_DIM), jnp.float32), -4.0, 4.0)


def draw_key_states(key, part):
    base_rows = key_base(key)
    return base_rows.astype(jnp.bfloat16)


def draw_queries(key, part):
    key = jax.random.fold_in(key, 5)
    drawn_rows = jnp.clip(jax.random.normal(key, (TOKENS, HEADS * HEAD_DIM), jnp.float32), -4.0, 4.0)
    return drawn_rows.astype(jnp.bfloat16)


def draw_selection(key, part):
    key = jax.random.fold_in(key, 11)
    noise_ints = jax.random.randint(key, (N_CTX, N_CTX), 0, 4096)
    col_ids = jnp.arange(N_CTX, dtype=jnp.int32)[None, :]
    row_ids = jnp.arange(N_CTX, dtype=jnp.int32)[:, None]
    ranking = noise_ints * N_CTX + col_ids + 1
    ranking = jnp.where(col_ids < row_ids, ranking, 0)
    ordered = jnp.argsort(-ranking, axis=1, stable=True).astype(jnp.int32)
    picked = jnp.where(col_ids < row_ids, ordered, -1).astype(jnp.int32)
    return picked.reshape(N_CTX * TILES_BLK, PICKS)


def block_levels(own_key, shape, split, smallest, largest):
    loudness, own = 1.0, jax.random.fold_in(own_key, 6)
    for position, blocks in split:
        heights = jnp.exp(jax.random.uniform(jax.random.fold_in(own, position), (blocks,), jnp.float32, smallest / len(split), largest / len(split)))
        loudness = loudness * jnp.repeat(heights, shape[position] // blocks).reshape([-1 if axis == position else 1 for axis in range(len(shape))])
    return loudness


def centred(key, shape, width, reach, cuts=(), held_as=jnp.bfloat16):
    gain = block_levels(key, shape, cuts, -0.22, 0.18) if cuts else 1.0
    array = jax.random.normal(key, shape, jnp.float32) * width * gain
    return jnp.minimum(jnp.maximum(array, -reach), reach).astype(held_as)


def setup_inputs(seed: int = 0) -> dict:
    keys = jax.random.split(jax.random.key(seed), 5)
    queries = draw_queries(jax.random.fold_in(keys[4], 71), 0)
    key_states = draw_key_states(jax.random.fold_in(keys[4], 71), 0)
    value_states = centred(keys[2], (TOKENS, HEADS * HEAD_DIM), 1.0, 4.0, ((0, 32), (1, 8)))
    selection = draw_selection(jax.random.fold_in(keys[4], 71), 0)
    return {"queries": queries, "key_states": key_states, "value_states": value_states, "selection": selection}


neg_large = -1e+30

def attend(query_rows, key_rows, value_rows, causal):
    scores = jnp.einsum('qhd,khd->hqk', query_rows.astype(jnp.float32), key_rows.astype(jnp.float32), precision=lax.Precision.HIGHEST)
    scores = scores * (1.0 / math.sqrt(query_rows.shape[2]))
    if causal:
        row_ids = lax.broadcasted_iota(jnp.int32, scores.shape, 1)
        col_ids = lax.broadcasted_iota(jnp.int32, scores.shape, 2)
        scores = jnp.where(col_ids <= row_ids, scores, neg_large)
    maximum = lax.optimization_barrier(jnp.max(scores, axis=2, keepdims=True))
    weights = jnp.exp(scores - maximum)
    summed = lax.optimization_barrier(jnp.sum(weights, axis=2, keepdims=True))
    probabilities = lax.optimization_barrier((weights / summed).astype(jnp.bfloat16))
    output = jnp.einsum('hqk,khd->qhd', probabilities.astype(jnp.float32), value_rows.astype(jnp.float32), precision=lax.Precision.HIGHEST)
    log_total = jnp.transpose(maximum[:, :, 0] + jnp.log(summed[:, :, 0]))
    return (output, log_total)

def combine(own_out, own_log, far_out, far_log, far_live):
    live_mask = far_live[:, :, None, None]
    far_masked = jnp.where(live_mask, far_log, neg_large)
    maximum = jnp.maximum(own_log, lax.optimization_barrier(jnp.max(far_masked, axis=1)))
    own_weight = jnp.exp(own_log - maximum)
    far_weight = jnp.where(live_mask, jnp.exp(far_masked - maximum[:, None]), 0.0)
    numerator = own_weight[..., None] * own_out + lax.optimization_barrier(jnp.sum(far_weight[..., None] * far_out, axis=1))
    denominator = own_weight + lax.optimization_barrier(jnp.sum(far_weight, axis=1))
    return numerator / denominator[..., None]

def reference(queries, key_states, value_states, selection):
    blocks = TOKENS // BLOCK
    tile_count = BLOCK // TILE

    def one_block(block_index):
        row_start = block_index * BLOCK
        query_block = lax.dynamic_slice_in_dim(queries, row_start, BLOCK, 0).reshape(BLOCK, HEADS, HEAD_DIM)
        key_block = lax.dynamic_slice_in_dim(key_states, row_start, BLOCK, 0).reshape(BLOCK, HEADS, HEAD_DIM)
        value_block = lax.dynamic_slice_in_dim(value_states, row_start, BLOCK, 0).reshape(BLOCK, HEADS, HEAD_DIM)
        own_out, own_log = attend(query_block, key_block, value_block, True)
        picked = lax.dynamic_slice_in_dim(selection, block_index * tile_count, tile_count, 0)
        tile_queries = query_block.reshape(tile_count, TILE, HEADS, HEAD_DIM)

        def one_tile(packed):
            tile_rows, tile_picks = packed
            out_list = []
            log_list = []
            for pick_rank in range(PICKS):
                source = (jnp.maximum(tile_picks[pick_rank], 0) * BLOCK).astype(jnp.int32)
                far_keys = lax.dynamic_slice_in_dim(key_states, source, BLOCK, 0).reshape(BLOCK, HEADS, HEAD_DIM)
                far_values = lax.dynamic_slice_in_dim(value_states, source, BLOCK, 0).reshape(BLOCK, HEADS, HEAD_DIM)
                part_out, part_log = attend(tile_rows, far_keys, far_values, False)
                part_out = lax.optimization_barrier(part_out.astype(jnp.bfloat16)).astype(jnp.float32)
                out_list.append(part_out)
                log_list.append(part_log)
            return (jnp.stack(out_list), jnp.stack(log_list))
        far_out, far_log = lax.map(one_tile, (tile_queries, picked))
        combined = combine(own_out.reshape(tile_count, TILE, HEADS, HEAD_DIM), own_log.reshape(tile_count, TILE, HEADS), far_out, far_log, picked >= 0)
        return combined.astype(jnp.bfloat16).reshape(BLOCK, HEADS * HEAD_DIM)
    result = lax.map(one_block, jnp.arange(blocks, dtype=jnp.int32))
    return result.reshape(TOKENS, HEADS * HEAD_DIM)
```

```python
import functools
import math

import jax
import jax.numpy as jnp
from jax import lax
from jax.experimental import pallas as pl
from jax.experimental.pallas import tpu as pltpu
from jax.sharding import PartitionSpec as P

HEAD_DIM = 128
TILE = 48
GROUP = 4
UNIT = 16
ROWS = 128
LAG = 2
AHEAD = 2
FLIGHT = 1
NEG = -1e30
SCALE2 = math.log2(math.e) / math.sqrt(HEAD_DIM)
MESH = pl.DeviceIdType.MESH


def loop(low, high, step):
    def once(i, carry):
        step(i)
        return carry

    lax.fori_loop(low, high, once, 0)


def softmax_parts(scores, values):
    top = jnp.max(scores, axis=1, keepdims=True)
    weights = jnp.exp2((scores - top) * SCALE2).astype(jnp.bfloat16)
    summed = jnp.dot(weights, values, preferred_element_type=jnp.float32)
    total = summed[:, HEAD_DIM:]
    return summed[:, :HEAD_DIM] / total, top * SCALE2 + jnp.log2(total)


def kernel(
    blocks, depth, sel, q, k_hbm, v_hbm, out,
    k, outgoing, arrived, parts, part_lse, back, back_lse, own, own_lse, final, vext, going, onehot, pick, dead, picked_lse,
    fwd_send, fwd_recv, out_send, out_recv, lse_send, lse_recv, z_send, z_recv, load_sem,
):
    me, z = lax.axis_index("ctx"), lax.axis_index("head")
    rows, width = q.shape
    heads = width // HEAD_DIM
    tiles = rows // TILE
    share = rows // depth

    barrier = pltpu.get_barrier_semaphore()
    loop(1, blocks, lambda i: pl.semaphore_signal(
        barrier, inc=1, device_id=(lax.rem(me + i, blocks), z), device_id_type=MESH))
    loop(1, depth, lambda i: pl.semaphore_signal(
        barrier, inc=1, device_id=(me, lax.rem(z + i, depth)), device_id_type=MESH))

    def columns(h):
        return pl.ds(pl.multiple_of(h * HEAD_DIM, HEAD_DIM), HEAD_DIM)

    load_k = pltpu.make_async_copy(k_hbm, k, load_sem.at[heads])
    load_v = [
        pltpu.make_async_copy(
            v_hbm.at[:, h * HEAD_DIM:(h + 1) * HEAD_DIM], vext.at[h, :, :HEAD_DIM], load_sem.at[h])
        for h in range(heads)
    ]
    for copy in [load_k] + load_v:
        copy.start()

    def shifted(size):
        return (lax.broadcasted_iota(jnp.int32, (TILE, size), 1)
                - lax.broadcasted_iota(jnp.int32, (TILE, size), 0))

    lanes = lax.broadcasted_iota(jnp.int32, (1, HEAD_DIM), 1)

    def choose(c):
        tile = jnp.int32(0)
        for t in range(tiles):
            tile += jnp.where((sel[t, 0] == c) | (sel[t, 1] == c), t, 0)
        here = pl.ds(pl.multiple_of(c * TILE, 16), TILE)
        going[here] = jnp.where(shifted(rows) == tile * TILE, 1.0, 0.0).astype(jnp.bfloat16)

    def select(t):
        for r in range(2):
            i, c = 2 * t + r, sel[t, r]
            here = pl.ds(pl.multiple_of(i * TILE, 16), TILE)
            onehot[here] = jnp.where(shifted(blocks * TILE) == c * TILE, 1.0, 0.0).astype(jnp.bfloat16)
            pick[pl.ds(i, 1)] = jnp.where(lanes == c, 1.0, 0.0)
            dead[pl.ds(i, 1)] = jnp.where(lanes * 0 + c < 0, NEG, 0.0)

    slots = 2 * GROUP
    quads = (me + slots - 1) // slots

    def gather(h):
        def one_quad(j):
            here = pl.ds(pl.multiple_of(j * slots * TILE, 16), slots * TILE)
            tiles_out = jnp.dot(going[here], q[:, columns(h)], preferred_element_type=jnp.float32)
            outgoing[h, pl.ds(j * slots, slots)] = tiles_out.astype(jnp.bfloat16).reshape(slots, TILE, HEAD_DIM)

        loop(0, quads, one_quad)

    loop(0, quads * slots, choose)
    loop(0, FLIGHT, gather)
    loop(0, quads * GROUP, select)

    def clear(c):
        for h in range(heads):
            back[h, c] = jnp.zeros((TILE, HEAD_DIM), jnp.bfloat16)
            back_lse[h, c] = jnp.zeros((1, HEAD_DIM), jnp.float32)

    loop(me, blocks, clear)

    for h in range(heads):
        vext[h, :, HEAD_DIM:] = jnp.ones((rows, HEAD_DIM), jnp.bfloat16)
    for copy in [load_k] + load_v:
        copy.wait()

    pl.semaphore_wait(barrier, blocks - 1 + depth - 1)

    def forward(h, c, slot):
        return pltpu.make_async_remote_copy(
            src_ref=outgoing.at[h, c], dst_ref=arrived.at[h, slot],
            send_sem=fwd_send.at[c], recv_sem=fwd_recv.at[h, slot],
            device_id=(c, z), device_id_type=MESH)

    def backward(h, b, slot):
        return pltpu.make_async_remote_copy(
            src_ref=parts.at[h, b], dst_ref=back.at[h, slot],
            send_sem=out_send.at[b], recv_sem=out_recv.at[h, slot],
            device_id=(b, z), device_id_type=MESH)

    def backward_lse(h, b, slot):
        return pltpu.make_async_remote_copy(
            src_ref=part_lse.at[h, b], dst_ref=back_lse.at[h, slot],
            send_sem=lse_send.at[b], recv_sem=lse_recv.at[h, slot],
            device_id=(b, z), device_id_type=MESH)

    def across(h, d):
        other = lax.rem(z + d, depth)
        return pltpu.make_async_remote_copy(
            src_ref=final.at[h, pl.ds(pl.multiple_of(other * share, 16), share)],
            dst_ref=out.at[:, columns(z * heads + h)],
            send_sem=z_send.at[h], recv_sem=z_recv.at[h],
            device_id=(me, other), device_id_type=MESH)

    def send_tiles(h):
        @pl.when(h > 0)
        def _():
            loop(0, me, lambda c: forward(h - 1, c, me).wait_send())

        loop(0, me, lambda i: forward(h, me - 1 - i, me).start())

    def parts_sent(h, low, high):
        def sent(b):
            backward(h, b, me).wait_send()
            backward_lse(h, b, me).wait_send()

        loop(low, high, sent)

    loop(0, FLIGHT, send_tiles)

    def attend_own(h):
        for r in range(rows // ROWS):
            low, high = r * ROWS, (r + 1) * ROWS
            scores = lax.dot_general(
                q[low:high, columns(h)], k[:high, columns(h)], (((1,), (1,)), ((), ())),
                preferred_element_type=jnp.float32)
            row_ids = low + lax.broadcasted_iota(jnp.int32, scores.shape, 0)
            col_ids = lax.broadcasted_iota(jnp.int32, scores.shape, 1)
            scores = jnp.where(col_ids <= row_ids, scores, NEG)
            own[h, low:high], own_lse[h, low:high] = softmax_parts(scores, vext[h, :high])

    lane = lax.broadcasted_iota(jnp.int32, (TILE, HEAD_DIM), 1)
    row = lax.broadcasted_iota(jnp.int32, (TILE, HEAD_DIM), 0)
    diagonal = lane == row

    def attend_far(h):
        loop(me + 1, blocks, lambda b: forward(h, b, b).wait_recv())

        @pl.when(h > 0)
        def _():
            parts_sent(h - 1, me + 1, blocks)

        def one_group(first):
            queries = arrived[h, pl.ds(first, GROUP)].reshape(GROUP * TILE, HEAD_DIM)
            scores = lax.dot_general(
                queries, k[:, columns(h)], (((1,), (1,)), ((), ())),
                preferred_element_type=jnp.float32)
            output, lse = softmax_parts(scores, vext[h])
            parts[h, pl.ds(first, GROUP)] = output.astype(jnp.bfloat16).reshape(GROUP, TILE, HEAD_DIM)
            for j in range(GROUP):
                part_lse[h, first + j] = jnp.sum(
                    jnp.where(diagonal, lse[j * TILE:(j + 1) * TILE], 0.0), axis=0, keepdims=True)

        def one_unit(i):
            first = blocks - UNIT * (i + 1)
            for g in range(UNIT // GROUP):
                one_group(first + g * GROUP)

            def send(b):
                backward(h, b, me).start()
                backward_lse(h, b, me).start()

            loop(jnp.maximum(first, me + 1), first + UNIT, send)

        loop(0, (blocks - 1 - me + UNIT - 1) // UNIT, one_unit)

    def combine(h):
        def arrive(c):
            backward(h, c, c).wait_recv()
            backward_lse(h, c, c).wait_recv()

        loop(0, me, arrive)
        picked_lse[...] = dead[...] + jnp.dot(
            pick[:, :blocks], back_lse[h].reshape(blocks, HEAD_DIM),
            precision=lax.Precision.HIGHEST, preferred_element_type=jnp.float32)

        def with_far(j):
            got = jnp.dot(
                onehot[pl.ds(pl.multiple_of(j * slots * TILE, 16), slots * TILE)],
                back[h].reshape(blocks * TILE, HEAD_DIM), preferred_element_type=jnp.float32)
            for t in range(GROUP):
                here = pl.ds(pl.multiple_of((GROUP * j + t) * TILE, 16), TILE)
                outputs, lses = [own[h, here]], [own_lse[h, here]]
                for r in range(2):
                    i = 2 * t + r
                    outputs.append(got[i * TILE:(i + 1) * TILE])
                    spread = jnp.where(diagonal, picked_lse[pl.ds(slots * j + i, 1)], 0.0)
                    lses.append(jnp.sum(spread, axis=1, keepdims=True))
                top = jnp.maximum(jnp.maximum(lses[0], lses[1]), lses[2])
                weights = [jnp.exp2(lse - top) for lse in lses]
                numerator = weights[0] * outputs[0] + weights[1] * outputs[1] + weights[2] * outputs[2]
                final[h, here] = (numerator / (weights[0] + weights[1] + weights[2])).astype(jnp.bfloat16)

        def alone(j):
            here = pl.ds(pl.multiple_of(j * GROUP * TILE, 16), GROUP * TILE)
            final[h, here] = own[h, here].astype(jnp.bfloat16)

        loop(0, quads, with_far)
        loop(quads, tiles // GROUP, alone)
        for d in range(1, depth):
            across(h, d).start()
        out[:, columns(z * heads + h)] = final[h, pl.ds(pl.multiple_of(z * share, 16), share)]

    loop(0, AHEAD, attend_own)

    def one_step(h):
        @pl.when(h + FLIGHT < heads)
        def _():
            gather(h + FLIGHT)
            send_tiles(h + FLIGHT)

        @pl.when(h < heads)
        def _():
            attend_far(h)

        @pl.when(h + AHEAD < heads)
        def _():
            attend_own(h + AHEAD)

        @pl.when(h >= LAG)
        def _():
            combine(h - LAG)

    loop(0, heads + LAG, one_step)

    loop(0, me, lambda c: forward(heads - 1, c, me).wait_send())
    parts_sent(heads - 1, me + 1, blocks)

    def drain(h):
        shares = final.at[h, :(depth - 1) * share]
        pltpu.make_async_copy(shares, shares, z_send.at[h]).wait()
        pltpu.make_async_copy(shares, shares, z_recv.at[h]).wait()

    loop(0, heads, drain)


def body(blocks, depth, queries, key_states, value_states, selection):
    rows, width = queries.shape
    heads = width // HEAD_DIM
    bf16, f32 = jnp.bfloat16, jnp.float32
    tile_set = pltpu.VMEM((heads, blocks, TILE, HEAD_DIM), bf16)
    lse_set = pltpu.VMEM((heads, blocks, 1, HEAD_DIM), f32)
    dma = pltpu.SemaphoreType.DMA
    vmem, anywhere = pl.BlockSpec(memory_space=pltpu.VMEM), pl.BlockSpec(memory_space=pl.ANY)
    return pl.pallas_call(
        functools.partial(kernel, blocks, depth),
        out_shape=jax.ShapeDtypeStruct((rows // depth, width * depth), bf16),
        in_specs=[pl.BlockSpec(memory_space=pltpu.SMEM), vmem, anywhere, anywhere],
        out_specs=vmem,
        scratch_shapes=[
            pltpu.VMEM((rows, width), bf16),
            tile_set, tile_set, tile_set, lse_set, tile_set, lse_set,
            pltpu.VMEM((heads, rows, HEAD_DIM), f32),
            pltpu.VMEM((heads, rows, HEAD_DIM), f32),
            pltpu.VMEM((heads, rows, HEAD_DIM), bf16),
            pltpu.VMEM((heads, rows, 2 * HEAD_DIM), bf16),
            pltpu.VMEM((blocks * TILE, rows), bf16),
            pltpu.VMEM((blocks * TILE, blocks * TILE), bf16),
            pltpu.VMEM((blocks, HEAD_DIM), f32),
            pltpu.VMEM((blocks, HEAD_DIM), f32),
            pltpu.VMEM((blocks, HEAD_DIM), f32),
            dma((blocks,)), dma((heads, blocks)), dma((blocks,)), dma((heads, blocks)),
            dma((blocks,)), dma((heads, blocks)), dma((heads,)), dma((heads,)),
            dma((heads + 1,)),
        ],
        compiler_params=pltpu.CompilerParams(
            collective_id=0, has_side_effects=True, vmem_limit_bytes=56 * 2**20),
    )(selection, queries, key_states, value_states)


def solution(mesh):
    placed = (P("ctx", "head"), P("ctx", "head"), P("ctx", "head"), P("ctx", None))
    return jax.shard_map(
        functools.partial(body, mesh.shape["ctx"], mesh.shape["head"]),
        mesh=mesh, in_specs=placed, out_specs=P(("ctx", "head"), None), check_vma=False)
```

```python
import functools
import math

import jax
import jax.numpy as jnp
from jax import lax
from jax.experimental import pallas as pl
from jax.experimental.pallas import tpu as pltpu
from jax.sharding import PartitionSpec as P

HEAD_DIM = 128
TILE = 48
GROUP = 4
UNIT = 16
ROWS = 128
LAG = 2
AHEAD = 2
FLIGHT = 1
NEG = -1e30
SCALE2 = math.log2(math.e) / math.sqrt(HEAD_DIM)
MESH = pl.DeviceIdType.MESH


def loop(low, high, step):
    def once(i, carry):
        step(i)
        return carry

    lax.fori_loop(low, high, once, 0)


def same(a, b):
    return jnp.maximum(1 - jnp.maximum(a - b, b - a), 0)


def by_index(index, count, leaf, fold=8):
    for a in range(0, count, fold):
        def some(_, a=a):
            for i in range(a, a + fold):
                loop(0, same(index, i), lambda _, i=i: leaf(i))

        loop(0, same(index // fold, a // fold), some)


def softmax_parts(scores, values):
    top = jnp.max(scores, axis=1, keepdims=True)
    weights = jnp.exp2((scores - top) * SCALE2).astype(jnp.bfloat16)
    summed = jnp.dot(weights, values, preferred_element_type=jnp.float32)
    total = summed[:, HEAD_DIM:]
    return summed[:, :HEAD_DIM] / total, top * SCALE2 + jnp.log2(total)


def kernel(
    blocks, depth, sel, q_hbm, k_hbm, v_hbm, out,
    q, k, outgoing, arrived, parts, part_lse, back, back_lse, own, own_lse, final, vext, going, onehot, pick, dead, picked_lse,
    fwd_send, fwd_recv, out_send, out_recv, lse_send, lse_recv, z_send, z_recv, load_sem,
):
    me, z = lax.axis_index("ctx"), lax.axis_index("head")
    rows, width = q.shape
    heads = width // HEAD_DIM
    tiles = rows // TILE
    share = rows // depth

    barrier = pltpu.get_barrier_semaphore()
    loop(1, blocks, lambda i: pl.semaphore_signal(
        barrier, inc=1, device_id=(lax.rem(me + i, blocks), z), device_id_type=MESH))
    loop(1, depth, lambda i: pl.semaphore_signal(
        barrier, inc=1, device_id=(me, lax.rem(z + i, depth)), device_id_type=MESH))

    def columns(h):
        return pl.ds(pl.multiple_of(h * HEAD_DIM, HEAD_DIM), HEAD_DIM)

    load_q = pltpu.make_async_copy(q_hbm, q, load_sem.at[heads + 1])
    load_k = pltpu.make_async_copy(k_hbm, k, load_sem.at[heads])
    load_v = [
        pltpu.make_async_copy(
            v_hbm.at[:, h * HEAD_DIM:(h + 1) * HEAD_DIM], vext.at[h, :, :HEAD_DIM], load_sem.at[h])
        for h in range(heads)
    ]
    for copy in [load_q, load_k] + load_v:
        copy.start()

    def shifted(size):
        return (lax.broadcasted_iota(jnp.int32, (TILE, size), 1)
                - lax.broadcasted_iota(jnp.int32, (TILE, size), 0))

    lanes = lax.broadcasted_iota(jnp.int32, (1, HEAD_DIM), 1)

    def choose(c):
        tile = jnp.int32(0)
        for t in range(tiles):
            tile += jnp.where((sel[t, 0] == c) | (sel[t, 1] == c), t, 0)
        here = pl.ds(pl.multiple_of(c * TILE, 16), TILE)
        going[here] = jnp.where(shifted(rows) == tile * TILE, 1.0, 0.0).astype(jnp.bfloat16)

    def select(t):
        for r in range(2):
            i, c = 2 * t + r, sel[t, r]
            here = pl.ds(pl.multiple_of(i * TILE, 16), TILE)
            onehot[here] = jnp.where(shifted(blocks * TILE) == c * TILE, 1.0, 0.0).astype(jnp.bfloat16)
            pick[pl.ds(i, 1)] = jnp.where(lanes == c, 1.0, 0.0)
            dead[pl.ds(i, 1)] = jnp.where(lanes * 0 + c < 0, NEG, 0.0)

    slots = 2 * GROUP
    quads = (me + slots - 1) // slots

    def gather(h):
        def one_quad(j):
            here = pl.ds(pl.multiple_of(j * slots * TILE, 16), slots * TILE)
            tiles_out = jnp.dot(going[here], q[:, columns(h)], preferred_element_type=jnp.float32)
            outgoing[h, pl.ds(j * slots, slots)] = tiles_out.astype(jnp.bfloat16).reshape(slots, TILE, HEAD_DIM)

        loop(0, quads, one_quad)

    loop(0, quads * slots, choose)
    load_q.wait()
    loop(0, FLIGHT, gather)
    loop(0, quads * GROUP, select)

    def clear(c):
        for h in range(heads):
            back[h, c] = jnp.zeros((TILE, HEAD_DIM), jnp.bfloat16)
            back_lse[h, c] = jnp.zeros((1, HEAD_DIM), jnp.float32)

    loop(me, blocks, clear)

    for h in range(heads):
        vext[h, :, HEAD_DIM:] = jnp.ones((rows, HEAD_DIM), jnp.bfloat16)
    for copy in [load_k] + load_v:
        copy.wait()

    pl.semaphore_wait(barrier, blocks - 1 + depth - 1)

    def forward(h, c, slot):
        return pltpu.make_async_remote_copy(
            src_ref=outgoing.at[h, c], dst_ref=arrived.at[h, slot],
            send_sem=fwd_send.at[h], recv_sem=fwd_recv.at[h],
            device_id=(c, z), device_id_type=MESH)

    def backward(h, b, slot):
        return pltpu.make_async_remote_copy(
            src_ref=parts.at[h, b], dst_ref=back.at[h, slot],
            send_sem=out_send.at[h], recv_sem=out_recv.at[h],
            device_id=(b, z), device_id_type=MESH)

    def backward_lse(h, b, slot):
        return pltpu.make_async_remote_copy(
            src_ref=part_lse.at[h, b], dst_ref=back_lse.at[h, slot],
            send_sem=lse_send.at[h], recv_sem=lse_recv.at[h],
            device_id=(b, z), device_id_type=MESH)

    def across(h, d):
        other = lax.rem(z + d, depth)
        return pltpu.make_async_remote_copy(
            src_ref=final.at[h, pl.ds(pl.multiple_of(other * share, 16), share)],
            dst_ref=out.at[:, columns(z * heads + h)],
            send_sem=z_send.at[h], recv_sem=z_recv.at[h],
            device_id=(me, other), device_id_type=MESH)

    def take(ref, low, high, send_sem, recv_sem):
        slots = ref.at[low:high]
        return pltpu.make_async_remote_copy(
            src_ref=slots, dst_ref=slots, send_sem=send_sem, recv_sem=recv_sem,
            device_id=(lax.rem(me + 1, blocks), z), device_id_type=MESH)

    def send_tiles(h):
        loop(0, me, lambda i: forward(h, me - 1 - i, me).start())

    loop(0, FLIGHT, send_tiles)

    def attend_own(h):
        for r in range(rows // ROWS):
            low, high = r * ROWS, (r + 1) * ROWS
            scores = lax.dot_general(
                q[low:high, columns(h)], k[:high, columns(h)], (((1,), (1,)), ((), ())),
                preferred_element_type=jnp.float32)
            row_ids = low + lax.broadcasted_iota(jnp.int32, scores.shape, 0)
            col_ids = lax.broadcasted_iota(jnp.int32, scores.shape, 1)
            scores = jnp.where(col_ids <= row_ids, scores, NEG)
            own[h, low:high], own_lse[h, low:high] = softmax_parts(scores, vext[h, :high])

    lane = lax.broadcasted_iota(jnp.int32, (TILE, HEAD_DIM), 1)
    row = lax.broadcasted_iota(jnp.int32, (TILE, HEAD_DIM), 0)
    diagonal = lane == row

    def attend_far(h):
        def arrive(m):
            if m + 1 < blocks:
                take(arrived.at[h], m + 1, blocks, fwd_send.at[h], fwd_recv.at[h]).wait_recv()

        by_index(me, blocks, arrive)

        def one_group(first):
            queries = arrived[h, pl.ds(first, GROUP)].reshape(GROUP * TILE, HEAD_DIM)
            scores = lax.dot_general(
                queries, k[:, columns(h)], (((1,), (1,)), ((), ())),
                preferred_element_type=jnp.float32)
            output, lse = softmax_parts(scores, vext[h])
            parts[h, pl.ds(first, GROUP)] = output.astype(jnp.bfloat16).reshape(GROUP, TILE, HEAD_DIM)
            for j in range(GROUP):
                part_lse[h, first + j] = jnp.sum(
                    jnp.where(diagonal, lse[j * TILE:(j + 1) * TILE], 0.0), axis=0, keepdims=True)

        def one_unit(i):
            first = blocks - UNIT * (i + 1)
            for g in range(UNIT // GROUP):
                one_group(first + g * GROUP)

            def send(b):
                backward(h, b, me).start()
                backward_lse(h, b, me).start()

            loop(jnp.maximum(first, me + 1), first + UNIT, send)

        loop(0, (blocks - 1 - me + UNIT - 1) // UNIT, one_unit)

    def combine(h):
        def arrive(m):
            if m:
                take(back.at[h], 0, m, out_send.at[h], out_recv.at[h]).wait_recv()
                take(back_lse.at[h], 0, m, lse_send.at[h], lse_recv.at[h]).wait_recv()

        by_index(me, blocks, arrive)
        picked_lse[...] = dead[...] + jnp.dot(
            pick[:, :blocks], back_lse[h].reshape(blocks, HEAD_DIM),
            precision=lax.Precision.HIGHEST, preferred_element_type=jnp.float32)

        def with_far(j):
            got = jnp.dot(
                onehot[pl.ds(pl.multiple_of(j * slots * TILE, 16), slots * TILE)],
                back[h].reshape(blocks * TILE, HEAD_DIM), preferred_element_type=jnp.float32)
            for t in range(GROUP):
                here = pl.ds(pl.multiple_of((GROUP * j + t) * TILE, 16), TILE)
                outputs, lses = [own[h, here]], [own_lse[h, here]]
                for r in range(2):
                    i = 2 * t + r
                    outputs.append(got[i * TILE:(i + 1) * TILE])
                    spread = jnp.where(diagonal, picked_lse[pl.ds(slots * j + i, 1)], 0.0)
                    lses.append(jnp.sum(spread, axis=1, keepdims=True))
                top = jnp.maximum(jnp.maximum(lses[0], lses[1]), lses[2])
                weights = [jnp.exp2(lse - top) for lse in lses]
                numerator = weights[0] * outputs[0] + weights[1] * outputs[1] + weights[2] * outputs[2]
                final[h, here] = (numerator / (weights[0] + weights[1] + weights[2])).astype(jnp.bfloat16)

        def alone(j):
            here = pl.ds(pl.multiple_of(j * GROUP * TILE, 16), GROUP * TILE)
            final[h, here] = own[h, here].astype(jnp.bfloat16)

        loop(0, quads, with_far)
        loop(quads, tiles // GROUP, alone)
        for d in range(1, depth):
            across(h, d).start()
        out[:, columns(z * heads + h)] = final[h, pl.ds(pl.multiple_of(z * share, 16), share)]

    loop(0, AHEAD, attend_own)

    def one_step(h):
        @pl.when(h + FLIGHT < heads)
        def _():
            gather(h + FLIGHT)
            send_tiles(h + FLIGHT)

        @pl.when(h >= LAG)
        def _():
            combine(h - LAG)

        @pl.when(h < heads)
        def _():
            attend_far(h)

        @pl.when(h + AHEAD < heads)
        def _():
            attend_own(h + AHEAD)

    loop(0, heads + LAG, one_step)

    def drain(h):
        def sent(m):
            if m:
                take(outgoing.at[h], 0, m, fwd_send.at[h], fwd_recv.at[h]).wait_send()
            if m + 1 < blocks:
                take(parts.at[h], m + 1, blocks, out_send.at[h], out_recv.at[h]).wait_send()
                take(part_lse.at[h], m + 1, blocks, lse_send.at[h], lse_recv.at[h]).wait_send()

        by_index(me, blocks, sent)
        others = take(final.at[h], 0, (depth - 1) * share, z_send.at[h], z_recv.at[h])
        others.wait_send()
        others.wait_recv()

    loop(0, heads, drain)


def body(blocks, depth, queries, key_states, value_states, selection):
    rows, width = queries.shape
    heads = width // HEAD_DIM
    bf16, f32 = jnp.bfloat16, jnp.float32
    tile_set = pltpu.VMEM((heads, blocks, TILE, HEAD_DIM), bf16)
    lse_set = pltpu.VMEM((heads, blocks, 1, HEAD_DIM), f32)
    dma = pltpu.SemaphoreType.DMA
    vmem, anywhere = pl.BlockSpec(memory_space=pltpu.VMEM), pl.BlockSpec(memory_space=pl.ANY)
    return pl.pallas_call(
        functools.partial(kernel, blocks, depth),
        out_shape=jax.ShapeDtypeStruct((rows // depth, width * depth), bf16),
        in_specs=[pl.BlockSpec(memory_space=pltpu.SMEM), anywhere, anywhere, anywhere],
        out_specs=vmem,
        scratch_shapes=[
            pltpu.VMEM((rows, width), bf16), pltpu.VMEM((rows, width), bf16),
            tile_set, tile_set, tile_set, lse_set, tile_set, lse_set,
            pltpu.VMEM((heads, rows, HEAD_DIM), f32),
            pltpu.VMEM((heads, rows, HEAD_DIM), f32),
            pltpu.VMEM((heads, rows, HEAD_DIM), bf16),
            pltpu.VMEM((heads, rows, 2 * HEAD_DIM), bf16),
            pltpu.VMEM((blocks * TILE, rows), bf16),
            pltpu.VMEM((blocks * TILE, blocks * TILE), bf16),
            pltpu.VMEM((blocks, HEAD_DIM), f32),
            pltpu.VMEM((blocks, HEAD_DIM), f32),
            pltpu.VMEM((blocks, HEAD_DIM), f32),
            *[dma((heads,)) for _ in range(8)],
            dma((heads + 2,)),
        ],
        compiler_params=pltpu.CompilerParams(
            collective_id=0, has_side_effects=True, vmem_limit_bytes=56 * 2**20),
    )(selection, queries, key_states, value_states)


def solution(mesh):
    placed = (P("ctx", "head"), P("ctx", "head"), P("ctx", "head"), P("ctx", None))
    return jax.shard_map(
        functools.partial(body, mesh.shape["ctx"], mesh.shape["head"]),
        mesh=mesh, in_specs=placed, out_specs=P(("ctx", "head"), None), check_vma=False)
```

```python
import functools
import math

import jax
import jax.numpy as jnp
from jax import lax
from jax.experimental import pallas as pl
from jax.experimental.pallas import tpu as pltpu
from jax.sharding import PartitionSpec as P

HEAD_DIM = 128
TILE = 48
GROUP = 4
UNIT = 16
ROWS = 128
LAG = 2
AHEAD = 2
FLIGHT = 1
NEG = -1e30
SCALE2 = math.log2(math.e) / math.sqrt(HEAD_DIM)
MESH = pl.DeviceIdType.MESH


def loop(low, high, step):
    def once(i, carry):
        step(i)
        return carry

    lax.fori_loop(low, high, once, 0)


def same(a, b):
    return jnp.maximum(1 - jnp.maximum(a - b, b - a), 0)


def by_index(index, count, leaf, fold=8):
    for a in range(0, count, fold):
        def some(_, a=a):
            for i in range(a, a + fold):
                loop(0, same(index, i), lambda _, i=i: leaf(i))

        loop(0, same(index // fold, a // fold), some)


def softmax_parts(scores, values):
    top = jnp.max(scores, axis=1, keepdims=True)
    weights = jnp.exp2((scores - top) * SCALE2).astype(jnp.bfloat16)
    summed = jnp.dot(weights, values, preferred_element_type=jnp.float32)
    total = summed[:, HEAD_DIM:]
    return summed[:, :HEAD_DIM] / total, top * SCALE2 + jnp.log2(total)


def kernel(
    blocks, depth, sel, q_hbm, k_hbm, v_hbm, out,
    q, k, outgoing, arrived, parts, part_lse, back, back_lse, own, own_lse, final, vext, going, onehot, pick, dead, picked_lse,
    fwd_send, fwd_recv, out_send, out_recv, lse_send, lse_recv, z_send, z_recv, load_sem,
):
    me, z = lax.axis_index("ctx"), lax.axis_index("head")
    rows, width = q.shape
    heads = width // HEAD_DIM
    tiles = rows // TILE
    share = rows // depth

    barrier = pltpu.get_barrier_semaphore()
    loop(1, blocks, lambda i: pl.semaphore_signal(
        barrier, inc=1, device_id=(lax.rem(me + i, blocks), z), device_id_type=MESH))
    loop(1, depth, lambda i: pl.semaphore_signal(
        barrier, inc=1, device_id=(me, lax.rem(z + i, depth)), device_id_type=MESH))

    def columns(h):
        return pl.ds(pl.multiple_of(h * HEAD_DIM, HEAD_DIM), HEAD_DIM)

    load_q = pltpu.make_async_copy(q_hbm, q, load_sem.at[heads + 1])
    load_k = pltpu.make_async_copy(k_hbm, k, load_sem.at[heads])
    load_v = [
        pltpu.make_async_copy(
            v_hbm.at[:, h * HEAD_DIM:(h + 1) * HEAD_DIM], vext.at[h, :, :HEAD_DIM], load_sem.at[h])
        for h in range(heads)
    ]
    for copy in [load_q, load_k] + load_v:
        copy.start()

    def shifted(size):
        return (lax.broadcasted_iota(jnp.int32, (TILE, size), 1)
                - lax.broadcasted_iota(jnp.int32, (TILE, size), 0))

    lanes = lax.broadcasted_iota(jnp.int32, (1, HEAD_DIM), 1)

    def choose(c):
        tile = jnp.int32(0)
        for t in range(tiles):
            tile += jnp.where((sel[t, 0] == c) | (sel[t, 1] == c), t, 0)
        here = pl.ds(pl.multiple_of(c * TILE, 16), TILE)
        going[here] = jnp.where(shifted(rows) == tile * TILE, 1.0, 0.0).astype(jnp.bfloat16)

    def select(t):
        for r in range(2):
            i, c = 2 * t + r, sel[t, r]
            here = pl.ds(pl.multiple_of(i * TILE, 16), TILE)
            onehot[here] = jnp.where(shifted(blocks * TILE) == c * TILE, 1.0, 0.0).astype(jnp.bfloat16)
            pick[pl.ds(i, 1)] = jnp.where(lanes == c, 1.0, 0.0)
            dead[pl.ds(i, 1)] = jnp.where(lanes * 0 + c < 0, NEG, 0.0)

    slots = 2 * GROUP
    quads = (me + slots - 1) // slots

    def gather(h):
        def one_quad(j):
            here = pl.ds(pl.multiple_of(j * slots * TILE, 16), slots * TILE)
            tiles_out = jnp.dot(going[here], q[:, columns(h)], preferred_element_type=jnp.float32)
            outgoing[h, pl.ds(j * slots, slots)] = tiles_out.astype(jnp.bfloat16).reshape(slots, TILE, HEAD_DIM)

        loop(0, quads, one_quad)

    loop(0, quads * slots, choose)
    load_q.wait()
    loop(0, FLIGHT, gather)
    pl.semaphore_wait(barrier, blocks - 1 + depth - 1)

    def forward(h, c, slot):
        return pltpu.make_async_remote_copy(
            src_ref=outgoing.at[h, c], dst_ref=arrived.at[h, slot],
            send_sem=fwd_send.at[h], recv_sem=fwd_recv.at[h],
            device_id=(c, z), device_id_type=MESH)

    def backward(h, b, slot):
        return pltpu.make_async_remote_copy(
            src_ref=parts.at[h, b], dst_ref=back.at[h, slot],
            send_sem=out_send.at[h], recv_sem=out_recv.at[h],
            device_id=(b, z), device_id_type=MESH)

    def backward_lse(h, b, slot):
        return pltpu.make_async_remote_copy(
            src_ref=part_lse.at[h, b], dst_ref=back_lse.at[h, slot],
            send_sem=lse_send.at[h], recv_sem=lse_recv.at[h],
            device_id=(b, z), device_id_type=MESH)

    def across(h, other):
        return pltpu.make_async_remote_copy(
            src_ref=final.at[h, pl.ds(pl.multiple_of(other * share, 16), share)],
            dst_ref=out.at[:, columns(z * heads + h)],
            send_sem=z_send.at[h], recv_sem=z_recv.at[h],
            device_id=(me, other), device_id_type=MESH)

    def take(ref, low, high, send_sem, recv_sem):
        slots = ref.at[low:high]
        return pltpu.make_async_remote_copy(
            src_ref=slots, dst_ref=slots, send_sem=send_sem, recv_sem=recv_sem,
            device_id=(lax.rem(me + 1, blocks), z), device_id_type=MESH)

    def send_tiles(h):
        loop(0, me, lambda i: forward(h, me - 1 - i, me).start())

    loop(0, FLIGHT, send_tiles)

    loop(0, quads * GROUP, select)

    def clear(c):
        for h in range(heads):
            back[h, c] = jnp.zeros((TILE, HEAD_DIM), jnp.bfloat16)
            back_lse[h, c] = jnp.zeros((1, HEAD_DIM), jnp.float32)

    loop(me, blocks, clear)

    for h in range(heads):
        vext[h, :, HEAD_DIM:] = jnp.ones((rows, HEAD_DIM), jnp.bfloat16)
    for copy in [load_k] + load_v:
        copy.wait()

    def attend_own(h):
        for r in range(rows // ROWS):
            low, high = r * ROWS, (r + 1) * ROWS
            scores = lax.dot_general(
                q[low:high, columns(h)], k[:high, columns(h)], (((1,), (1,)), ((), ())),
                preferred_element_type=jnp.float32)
            row_ids = low + lax.broadcasted_iota(jnp.int32, scores.shape, 0)
            col_ids = lax.broadcasted_iota(jnp.int32, scores.shape, 1)
            scores = jnp.where(col_ids <= row_ids, scores, NEG)
            own[h, low:high], own_lse[h, low:high] = softmax_parts(scores, vext[h, :high])

    lane = lax.broadcasted_iota(jnp.int32, (TILE, HEAD_DIM), 1)
    row = lax.broadcasted_iota(jnp.int32, (TILE, HEAD_DIM), 0)
    diagonal = lane == row

    def attend_far(h):
        def arrive(m):
            if m + 1 < blocks:
                take(arrived.at[h], m + 1, blocks, fwd_send.at[h], fwd_recv.at[h]).wait_recv()

        by_index(me, blocks, arrive)

        def one_group(first):
            queries = arrived[h, pl.ds(first, GROUP)].reshape(GROUP * TILE, HEAD_DIM)
            scores = lax.dot_general(
                queries, k[:, columns(h)], (((1,), (1,)), ((), ())),
                preferred_element_type=jnp.float32)
            output, lse = softmax_parts(scores, vext[h])
            parts[h, pl.ds(first, GROUP)] = output.astype(jnp.bfloat16).reshape(GROUP, TILE, HEAD_DIM)
            for j in range(GROUP):
                part_lse[h, first + j] = jnp.sum(
                    jnp.where(diagonal, lse[j * TILE:(j + 1) * TILE], 0.0), axis=0, keepdims=True)

        def one_unit(i):
            first = blocks - UNIT * (i + 1)
            for g in range(UNIT // GROUP):
                one_group(first + g * GROUP)

            def send(b):
                backward(h, b, me).start()
                backward_lse(h, b, me).start()

            loop(jnp.maximum(first, me + 1), first + UNIT, send)

        loop(0, (blocks - 1 - me + UNIT - 1) // UNIT, one_unit)

    def combine(h):
        def arrive(m):
            if m:
                take(back.at[h], 0, m, out_send.at[h], out_recv.at[h]).wait_recv()
                take(back_lse.at[h], 0, m, lse_send.at[h], lse_recv.at[h]).wait_recv()

        by_index(me, blocks, arrive)
        picked_lse[...] = dead[...] + jnp.dot(
            pick[:, :blocks], back_lse[h].reshape(blocks, HEAD_DIM),
            precision=lax.Precision.HIGHEST, preferred_element_type=jnp.float32)

        def with_far(j):
            got = jnp.dot(
                onehot[pl.ds(pl.multiple_of(j * slots * TILE, 16), slots * TILE)],
                back[h].reshape(blocks * TILE, HEAD_DIM), preferred_element_type=jnp.float32)
            for t in range(GROUP):
                here = pl.ds(pl.multiple_of((GROUP * j + t) * TILE, 16), TILE)
                outputs, lses = [own[h, here]], [own_lse[h, here]]
                for r in range(2):
                    i = 2 * t + r
                    outputs.append(got[i * TILE:(i + 1) * TILE])
                    spread = jnp.where(diagonal, picked_lse[pl.ds(slots * j + i, 1)], 0.0)
                    lses.append(jnp.sum(spread, axis=1, keepdims=True))
                top = jnp.maximum(jnp.maximum(lses[0], lses[1]), lses[2])
                weights = [jnp.exp2(lse - top) for lse in lses]
                numerator = weights[0] * outputs[0] + weights[1] * outputs[1] + weights[2] * outputs[2]
                final[h, here] = (numerator / (weights[0] + weights[1] + weights[2])).astype(jnp.bfloat16)

        def alone(j):
            here = pl.ds(pl.multiple_of(j * GROUP * TILE, 16), GROUP * TILE)
            final[h, here] = own[h, here].astype(jnp.bfloat16)

        def one_quad(i):
            j = lax.rem(z // 2 + i + 1, tiles // GROUP)

            @pl.when(j < quads)
            def _():
                with_far(j)

            @pl.when(j >= quads)
            def _():
                alone(j)

            def send(other):
                @pl.when(other != z)
                def _():
                    across(h, other).start()

            shares = GROUP * TILE // share
            loop(shares * j, shares * (j + 1), send)

        loop(0, tiles // GROUP, one_quad)
        out[:, columns(z * heads + h)] = final[h, pl.ds(pl.multiple_of(z * share, 16), share)]

    loop(0, AHEAD, attend_own)

    def one_step(h):
        @pl.when(h + FLIGHT < heads)
        def _():
            gather(h + FLIGHT)
            send_tiles(h + FLIGHT)

        @pl.when(h >= LAG)
        def _():
            combine(h - LAG)

        @pl.when(h < heads)
        def _():
            attend_far(h)

        @pl.when(h + AHEAD < heads)
        def _():
            attend_own(h + AHEAD)

    loop(0, heads + LAG, one_step)

    def drain(h):
        def sent(m):
            if m:
                take(outgoing.at[h], 0, m, fwd_send.at[h], fwd_recv.at[h]).wait_send()
            if m + 1 < blocks:
                take(parts.at[h], m + 1, blocks, out_send.at[h], out_recv.at[h]).wait_send()
                take(part_lse.at[h], m + 1, blocks, lse_send.at[h], lse_recv.at[h]).wait_send()

        by_index(me, blocks, sent)
        others = take(final.at[h], 0, (depth - 1) * share, z_send.at[h], z_recv.at[h])
        others.wait_send()
        others.wait_recv()

    loop(0, heads, drain)


def body(blocks, depth, queries, key_states, value_states, selection):
    rows, width = queries.shape
    heads = width // HEAD_DIM
    bf16, f32 = jnp.bfloat16, jnp.float32
    tile_set = pltpu.VMEM((heads, blocks, TILE, HEAD_DIM), bf16)
    lse_set = pltpu.VMEM((heads, blocks, 1, HEAD_DIM), f32)
    dma = pltpu.SemaphoreType.DMA
    vmem, anywhere = pl.BlockSpec(memory_space=pltpu.VMEM), pl.BlockSpec(memory_space=pl.ANY)
    return pl.pallas_call(
        functools.partial(kernel, blocks, depth),
        out_shape=jax.ShapeDtypeStruct((rows // depth, width * depth), bf16),
        in_specs=[pl.BlockSpec(memory_space=pltpu.SMEM), anywhere, anywhere, anywhere],
        out_specs=vmem,
        scratch_shapes=[
            pltpu.VMEM((rows, width), bf16), pltpu.VMEM((rows, width), bf16),
            tile_set, tile_set, tile_set, lse_set, tile_set, lse_set,
            pltpu.VMEM((heads, rows, HEAD_DIM), f32),
            pltpu.VMEM((heads, rows, HEAD_DIM), f32),
            pltpu.VMEM((heads, rows, HEAD_DIM), bf16),
            pltpu.VMEM((heads, rows, 2 * HEAD_DIM), bf16),
            pltpu.VMEM((blocks * TILE, rows), bf16),
            pltpu.VMEM((blocks * TILE, blocks * TILE), bf16),
            pltpu.VMEM((blocks, HEAD_DIM), f32),
            pltpu.VMEM((blocks, HEAD_DIM), f32),
            pltpu.VMEM((blocks, HEAD_DIM), f32),
            *[dma((heads,)) for _ in range(8)],
            dma((heads + 2,)),
        ],
        compiler_params=pltpu.CompilerParams(
            collective_id=0, has_side_effects=True, vmem_limit_bytes=56 * 2**20),
    )(selection, queries, key_states, value_states)


def solution(mesh):
    placed = (P("ctx", "head"), P("ctx", "head"), P("ctx", "head"), P("ctx", None))
    return jax.shard_map(
        functools.partial(body, mesh.shape["ctx"], mesh.shape["head"]),
        mesh=mesh, in_specs=placed, out_specs=P(("ctx", "head"), None), check_vma=False)
```

```python
import functools
import math

import jax
import jax.numpy as jnp
from jax import lax
from jax.experimental import pallas as pl
from jax.experimental.pallas import tpu as pltpu
from jax.sharding import PartitionSpec as P

HEAD_DIM = 128
TILE = 48
GROUP = 4
UNIT = 16
ROWS = 128
LAG = 2
AHEAD = 2
FLIGHT = 1
NEG = -1e30
SCALE2 = math.log2(math.e) / math.sqrt(HEAD_DIM)
MESH = pl.DeviceIdType.MESH


def loop(low, high, step):
    def once(i, carry):
        step(i)
        return carry

    lax.fori_loop(low, high, once, 0)


def same(a, b):
    return jnp.maximum(1 - jnp.maximum(a - b, b - a), 0)


def by_index(index, count, leaf, fold=8):
    for a in range(0, count, fold):
        def some(_, a=a):
            for i in range(a, a + fold):
                loop(0, same(index, i), lambda _, i=i: leaf(i))

        loop(0, same(index // fold, a // fold), some)


def softmax_parts(scores, values):
    top = jnp.max(scores, axis=1, keepdims=True)
    weights = jnp.exp2((scores - top) * SCALE2).astype(jnp.bfloat16)
    summed = jnp.dot(weights, values, preferred_element_type=jnp.float32)
    total = summed[:, HEAD_DIM:]
    return summed[:, :HEAD_DIM] / total, top * SCALE2 + jnp.log2(total)


def kernel(
    blocks, depth, sel, q_hbm, k_hbm, v_hbm, out,
    q, k, outgoing, arrived, parts, part_lse, back, back_lse, own, own_lse, final, vext, going, onehot, pick, dead, picked_lse,
    fwd_send, fwd_recv, out_send, out_recv, lse_send, lse_recv, z_send, z_recv, load_sem,
):
    me, z = lax.axis_index("ctx"), lax.axis_index("head")
    rows, width = q.shape
    heads = width // HEAD_DIM
    tiles = rows // TILE
    share = rows // depth

    barrier = pltpu.get_barrier_semaphore()
    loop(1, blocks, lambda i: pl.semaphore_signal(
        barrier, inc=1, device_id=(lax.rem(me + i, blocks), z), device_id_type=MESH))
    loop(1, depth, lambda i: pl.semaphore_signal(
        barrier, inc=1, device_id=(me, lax.rem(z + i, depth)), device_id_type=MESH))

    def columns(h):
        return pl.ds(pl.multiple_of(h * HEAD_DIM, HEAD_DIM), HEAD_DIM)

    load_q = pltpu.make_async_copy(q_hbm, q, load_sem.at[heads + 1])
    load_k = pltpu.make_async_copy(k_hbm, k, load_sem.at[heads])
    load_v = [
        pltpu.make_async_copy(
            v_hbm.at[:, h * HEAD_DIM:(h + 1) * HEAD_DIM], vext.at[h, :, :HEAD_DIM], load_sem.at[h])
        for h in range(heads)
    ]
    for copy in [load_q, load_k] + load_v:
        copy.start()

    def shifted(size):
        return (lax.broadcasted_iota(jnp.int32, (TILE, size), 1)
                - lax.broadcasted_iota(jnp.int32, (TILE, size), 0))

    lanes = lax.broadcasted_iota(jnp.int32, (1, HEAD_DIM), 1)

    def choose(c):
        tile = jnp.int32(0)
        for t in range(tiles):
            tile += jnp.where((sel[t, 0] == c) | (sel[t, 1] == c), t, 0)
        here = pl.ds(pl.multiple_of(c * TILE, 16), TILE)
        going[here] = jnp.where(shifted(rows) == tile * TILE, 1.0, 0.0).astype(jnp.bfloat16)

    def select(t):
        for r in range(2):
            i, c = 2 * t + r, sel[t, r]
            here = pl.ds(pl.multiple_of(i * TILE, 16), TILE)
            onehot[here] = jnp.where(shifted(blocks * TILE) == c * TILE, 1.0, 0.0).astype(jnp.bfloat16)
            pick[pl.ds(i, 1)] = jnp.where(lanes == c, 1.0, 0.0)
            dead[pl.ds(i, 1)] = jnp.where(lanes * 0 + c < 0, NEG, 0.0)

    slots = 2 * GROUP
    quads = (me + slots - 1) // slots

    def gather(h):
        def one_quad(j):
            here = pl.ds(pl.multiple_of(j * slots * TILE, 16), slots * TILE)
            tiles_out = jnp.dot(going[here], q[:, columns(h)], preferred_element_type=jnp.float32)
            outgoing[h, pl.ds(j * slots, slots)] = tiles_out.astype(jnp.bfloat16).reshape(slots, TILE, HEAD_DIM)

        loop(0, quads, one_quad)

    loop(0, quads * slots, choose)
    load_q.wait()
    loop(0, FLIGHT, gather)
    pl.semaphore_wait(barrier, blocks - 1 + depth - 1)

    def forward(h, c, slot):
        return pltpu.make_async_remote_copy(
            src_ref=outgoing.at[h, c], dst_ref=arrived.at[h, slot],
            send_sem=fwd_send.at[h], recv_sem=fwd_recv.at[h],
            device_id=(c, z), device_id_type=MESH)

    def backward(h, b, slot):
        return pltpu.make_async_remote_copy(
            src_ref=parts.at[h, b], dst_ref=back.at[h, slot],
            send_sem=out_send.at[h], recv_sem=out_recv.at[h],
            device_id=(b, z), device_id_type=MESH)

    def backward_lse(h, b, slot):
        return pltpu.make_async_remote_copy(
            src_ref=part_lse.at[h, b], dst_ref=back_lse.at[h, slot],
            send_sem=lse_send.at[h], recv_sem=lse_recv.at[h],
            device_id=(b, z), device_id_type=MESH)

    def across(h, other):
        return pltpu.make_async_remote_copy(
            src_ref=final.at[h, pl.ds(pl.multiple_of(other * share, 16), share)],
            dst_ref=out.at[:, columns(z * heads + h)],
            send_sem=z_send.at[h], recv_sem=z_recv.at[h],
            device_id=(me, other), device_id_type=MESH)

    def take(ref, low, high, send_sem, recv_sem):
        slots = ref.at[low:high]
        return pltpu.make_async_remote_copy(
            src_ref=slots, dst_ref=slots, send_sem=send_sem, recv_sem=recv_sem,
            device_id=(lax.rem(me + 1, blocks), z), device_id_type=MESH)

    def send_tiles(h):
        loop(0, me, lambda i: forward(h, me - 1 - i, me).start())

    loop(0, FLIGHT, send_tiles)
    gather(FLIGHT)
    send_tiles(FLIGHT)

    loop(0, quads * GROUP, select)

    def clear(c):
        for h in range(heads):
            back[h, c] = jnp.zeros((TILE, HEAD_DIM), jnp.bfloat16)
            back_lse[h, c] = jnp.zeros((1, HEAD_DIM), jnp.float32)

    loop(me, blocks, clear)

    for h in range(heads):
        vext[h, :, HEAD_DIM:] = jnp.ones((rows, HEAD_DIM), jnp.bfloat16)
    for copy in [load_k] + load_v:
        copy.wait()

    def attend_own(h):
        for r in range(rows // ROWS):
            low, high = r * ROWS, (r + 1) * ROWS
            scores = lax.dot_general(
                q[low:high, columns(h)], k[:high, columns(h)], (((1,), (1,)), ((), ())),
                preferred_element_type=jnp.float32)
            row_ids = low + lax.broadcasted_iota(jnp.int32, scores.shape, 0)
            col_ids = lax.broadcasted_iota(jnp.int32, scores.shape, 1)
            scores = jnp.where(col_ids <= row_ids, scores, NEG)
            own[h, low:high], own_lse[h, low:high] = softmax_parts(scores, vext[h, :high])

    lane = lax.broadcasted_iota(jnp.int32, (TILE, HEAD_DIM), 1)
    row = lax.broadcasted_iota(jnp.int32, (TILE, HEAD_DIM), 0)
    diagonal = lane == row

    def attend_far(h):
        def arrive(m):
            if m + 1 < blocks:
                take(arrived.at[h], m + 1, blocks, fwd_send.at[h], fwd_recv.at[h]).wait_recv()

        by_index(me, blocks, arrive)

        def one_group(first):
            queries = arrived[h, pl.ds(first, GROUP)].reshape(GROUP * TILE, HEAD_DIM)
            scores = lax.dot_general(
                queries, k[:, columns(h)], (((1,), (1,)), ((), ())),
                preferred_element_type=jnp.float32)
            output, lse = softmax_parts(scores, vext[h])
            parts[h, pl.ds(first, GROUP)] = output.astype(jnp.bfloat16).reshape(GROUP, TILE, HEAD_DIM)
            for j in range(GROUP):
                part_lse[h, first + j] = jnp.sum(
                    jnp.where(diagonal, lse[j * TILE:(j + 1) * TILE], 0.0), axis=0, keepdims=True)

        def one_unit(i):
            first = blocks - UNIT * (i + 1)
            for g in range(UNIT // GROUP):
                one_group(first + g * GROUP)

            def send(b):
                backward(h, b, me).start()
                backward_lse(h, b, me).start()

            loop(jnp.maximum(first, me + 1), first + UNIT, send)

        loop(0, (blocks - 1 - me + UNIT - 1) // UNIT, one_unit)

    def combine(h):
        def arrive(m):
            if m:
                take(back.at[h], 0, m, out_send.at[h], out_recv.at[h]).wait_recv()
                take(back_lse.at[h], 0, m, lse_send.at[h], lse_recv.at[h]).wait_recv()

        by_index(me, blocks, arrive)
        picked_lse[...] = dead[...] + jnp.dot(
            pick[:, :blocks], back_lse[h].reshape(blocks, HEAD_DIM),
            precision=lax.Precision.HIGHEST, preferred_element_type=jnp.float32)

        def with_far(j):
            got = jnp.dot(
                onehot[pl.ds(pl.multiple_of(j * slots * TILE, 16), slots * TILE)],
                back[h].reshape(blocks * TILE, HEAD_DIM), preferred_element_type=jnp.float32)
            for t in range(GROUP):
                here = pl.ds(pl.multiple_of((GROUP * j + t) * TILE, 16), TILE)
                outputs, lses = [own[h, here]], [own_lse[h, here]]
                for r in range(2):
                    i = 2 * t + r
                    outputs.append(got[i * TILE:(i + 1) * TILE])
                    spread = jnp.where(diagonal, picked_lse[pl.ds(slots * j + i, 1)], 0.0)
                    lses.append(jnp.sum(spread, axis=1, keepdims=True))
                top = jnp.maximum(jnp.maximum(lses[0], lses[1]), lses[2])
                weights = [jnp.exp2(lse - top) for lse in lses]
                numerator = weights[0] * outputs[0] + weights[1] * outputs[1] + weights[2] * outputs[2]
                final[h, here] = (numerator / (weights[0] + weights[1] + weights[2])).astype(jnp.bfloat16)

        def alone(j):
            here = pl.ds(pl.multiple_of(j * GROUP * TILE, 16), GROUP * TILE)
            final[h, here] = own[h, here].astype(jnp.bfloat16)

        def one_quad(i):
            j = lax.rem(z // 2 + i + 1, tiles // GROUP)

            @pl.when(j < quads)
            def _():
                with_far(j)

            @pl.when(j >= quads)
            def _():
                alone(j)

            def send(other):
                @pl.when(other != z)
                def _():
                    across(h, other).start()

            shares = GROUP * TILE // share
            loop(shares * j, shares * (j + 1), send)

        loop(0, tiles // GROUP, one_quad)
        out[:, columns(z * heads + h)] = final[h, pl.ds(pl.multiple_of(z * share, 16), share)]

    loop(0, AHEAD, attend_own)

    def one_step(h):
        @pl.when((h > 0) & (h + FLIGHT < heads))
        def _():
            gather(h + FLIGHT)
            send_tiles(h + FLIGHT)

        @pl.when(h >= LAG)
        def _():
            combine(h - LAG)

        @pl.when(h < heads)
        def _():
            attend_far(h)

        @pl.when(h + AHEAD < heads)
        def _():
            attend_own(h + AHEAD)

    loop(0, heads + LAG, one_step)

    def drain(h):
        def sent(m):
            if m:
                take(outgoing.at[h], 0, m, fwd_send.at[h], fwd_recv.at[h]).wait_send()
            if m + 1 < blocks:
                take(parts.at[h], m + 1, blocks, out_send.at[h], out_recv.at[h]).wait_send()
                take(part_lse.at[h], m + 1, blocks, lse_send.at[h], lse_recv.at[h]).wait_send()

        by_index(me, blocks, sent)
        others = take(final.at[h], 0, (depth - 1) * share, z_send.at[h], z_recv.at[h])
        others.wait_send()
        others.wait_recv()

    loop(0, heads, drain)


def body(blocks, depth, queries, key_states, value_states, selection):
    rows, width = queries.shape
    heads = width // HEAD_DIM
    bf16, f32 = jnp.bfloat16, jnp.float32
    tile_set = pltpu.VMEM((heads, blocks, TILE, HEAD_DIM), bf16)
    lse_set = pltpu.VMEM((heads, blocks, 1, HEAD_DIM), f32)
    dma = pltpu.SemaphoreType.DMA
    vmem, anywhere = pl.BlockSpec(memory_space=pltpu.VMEM), pl.BlockSpec(memory_space=pl.ANY)
    return pl.pallas_call(
        functools.partial(kernel, blocks, depth),
        out_shape=jax.ShapeDtypeStruct((rows // depth, width * depth), bf16),
        in_specs=[pl.BlockSpec(memory_space=pltpu.SMEM), anywhere, anywhere, anywhere],
        out_specs=vmem,
        scratch_shapes=[
            pltpu.VMEM((rows, width), bf16), pltpu.VMEM((rows, width), bf16),
            tile_set, tile_set, tile_set, lse_set, tile_set, lse_set,
            pltpu.VMEM((heads, rows, HEAD_DIM), f32),
            pltpu.VMEM((heads, rows, HEAD_DIM), f32),
            pltpu.VMEM((heads, rows, HEAD_DIM), bf16),
            pltpu.VMEM((heads, rows, 2 * HEAD_DIM), bf16),
            pltpu.VMEM((blocks * TILE, rows), bf16),
            pltpu.VMEM((blocks * TILE, blocks * TILE), bf16),
            pltpu.VMEM((blocks, HEAD_DIM), f32),
            pltpu.VMEM((blocks, HEAD_DIM), f32),
            pltpu.VMEM((blocks, HEAD_DIM), f32),
            *[dma((heads,)) for _ in range(8)],
            dma((heads + 2,)),
        ],
        compiler_params=pltpu.CompilerParams(
            collective_id=0, has_side_effects=True, vmem_limit_bytes=56 * 2**20),
    )(selection, queries, key_states, value_states)


def solution(mesh):
    placed = (P("ctx", "head"), P("ctx", "head"), P("ctx", "head"), P("ctx", None))
    return jax.shard_map(
        functools.partial(body, mesh.shape["ctx"], mesh.shape["head"]),
        mesh=mesh, in_specs=placed, out_specs=P(("ctx", "head"), None), check_vma=False)
```
